32 devices in a mesh: req: 8 (over y, x, core), tp: 4 (over z).
Axes of the slice: x: 2, y: 2, z: 4, core: 2. Of those that a mesh axis runs over, the one named last changes fastest.
Arguments:
- embeds: bfloat16 [2048, 2048], P(('req', 'tp')), may hold values from -25 to 25
- input_norm_gain: float32 [2048], replicated, may hold values from 0.25 to 1.75
- input_norm_bias: float32 [2048], replicated, may hold values from -3 to 3
- joined_projection_weight: bfloat16 [2048, 6144], P(None, 'tp'), may hold values from -0.125 to 0.125
- joined_projection_bias: float32 [6144], P('tp'), may hold values from -3 to 3
- adapter_down_weight: bfloat16 [4, 2048, 16], replicated, may hold values from -0.125 to 0.125
- adapter_up_weight: bfloat16 [4, 16, 6144], P(None, None, 'tp'), may hold values from -1.5 to 1.5
- attention_out_weight: bfloat16 [2048, 2048], P('tp'), may hold values from -0.125 to 0.125
- attention_out_bias: float32 [2048], replicated, may hold values from -3 to 3
- post_attention_norm_gain: float32 [2048], replicated, may hold values from 0.4 to 1.6
- post_attention_norm_bias: float32 [2048], replicated, may hold values from -3 to 3
- feedforward_up_weight: bfloat16 [2048, 4096], P(None, 'tp'), may hold values from -0.125 to 0.125
- feedforward_up_bias: float32 [4096], P('tp'), may hold values from -3 to 3
- feedforward_down_weight: bfloat16 [4096, 2048], P('tp'), may hold values from -0.09375 to 0.09375
- feedforward_down_bias: float32 [2048], replicated, may hold values from -3 to 3
- stored_keys: bfloat16 [8, 1024, 2048], P('req', None, 'tp'), may hold values from -400 to 400
- stored_values: bfloat16 [8, 1024, 2048], P('req', None, 'tp'), may hold values from -6 to 6
- stored_length: int32 [8], P('req'), may hold values from 2 to 1024, as said below
- tenant_first_request: int32 [3], replicated, may hold values from 1 to 7, as said below
- accept: int32 [2048], P(('req', 'tp')), may hold values 0 or 1
- replacement_token_index: int32 [2048], P('req'), may hold values from 0 to 50175, as said below
- word_embedding_table: bfloat16 [50176, 2048], P('req', 'tp'), may hold values from -6 to 6
Outputs:
- denoised: bfloat16 [2048, 2048], P(('req', 'tp'))
The draws below stay inside these ranges and needn't reach their ends.
Inputs may be any that keep to these rules, and one draw needn't show every extreme that they name: `stored_length`: one request has exactly 1024 cached positions. `tenant_first_request`: strictly increasing. `replacement_token_index`: of the 256 ids of one index of req, at most 96 lie in the rows o * 6272 to (o + 1) * 6272 - 1 of any one index o of req; one index o receives exactly 96 from every index of req, and every other index receives about equally many.
All inputs are finite; a program needn't handle non-finite values. No bound on the sum of `accept` on one device may be relied on, other than what follows from the above.
Results may differ from the reference program's by a relative error of at most 0.04.
Values may be sent and summed in bfloat16 or wider, within the bound.
A program may use at most 128 MiB of HBM per device.

```python
import math
import jax
import jax.numpy as jnp
from jax import lax

MODEL_WIDTH = 2048
H = 16
HD = 128
FF = 4096
VROW = 6272
ADAPTER_RANK = 16
TENANT_COUNT = 4
BLK = 256
CMAX = 1024
REQS = 8
TOK_DEV = 256
TOKENS = 2048
V = 50176
CAP = 96
N_REQ = 8
N_TP = 4


def cache_lengths(key):
    base = jax.random.fold_in(key, 101)
    key_one, key_two, key_three = jax.random.split(base, 3)
    first_factor = jax.random.randint(key_one, (REQS,), 0, CMAX - 1)
    second_factor = jax.random.randint(key_two, (REQS,), 0, CMAX - 1)
    lengths = 2 + first_factor * second_factor // (CMAX - 1)
    longest = jax.random.randint(key_three, (), 0, REQS)
    return jnp.where(jnp.arange(REQS) == longest, CMAX, lengths).astype(jnp.int32)


def draw_stored_length(key, part):
    return cache_lengths(key)


def draw_stored_keys(key, part):
    base = jax.random.fold_in(key, 202)
    key_one = jax.random.fold_in(base, 0)
    key_four = jax.random.fold_in(base, 3)
    key_five = jax.random.fold_in(base, 4)
    values = jax.random.normal(key_one, (REQS, CMAX, MODEL_WIDTH), jnp.float32)
    lengths = cache_lengths(key)[:, None, None]
    positions = jnp.arange(CMAX)[None, :, None]
    early = jax.random.randint(key_four, (REQS, 1, 1), 0, jnp.maximum(1, lengths - 600))
    far = 6.0 * jnp.clip(jax.random.normal(key_five, (REQS, 1, MODEL_WIDTH), jnp.float32), -4.5, 4.5)
    values = jnp.where(positions == early, far, values)
    return values.astype(jnp.bfloat16)


def draw_tenant_first_request(key, part):
    base = jax.random.fold_in(key, 303)
    chosen = jax.random.permutation(base, REQS - 1)[:TENANT_COUNT - 1] + 1
    return jnp.sort(chosen).astype(jnp.int32)


def draw_replacement_token_index(key, part):
    base = jax.random.fold_in(key, 404)
    key_one, key_two, key_three, key_four = jax.random.split(base, 4)
    hottest = jax.random.randint(key_one, (), 0, N_REQ)
    ranks = jax.vmap(lambda single: jax.random.permutation(single, TOK_DEV))(jax.random.split(key_two, N_REQ))
    offsets = jax.random.randint(key_three, (N_REQ, 1), 0, N_REQ - 1)
    others = (ranks - CAP + offsets) % (N_REQ - 1)
    others = others + (others >= hottest).astype(jnp.int32)
    owners = jnp.where(ranks < CAP, hottest, others)
    within = jax.random.randint(key_four, (N_REQ, TOK_DEV), 0, VROW)
    return (owners * VROW + within).reshape(TOKENS).astype(jnp.int32)


def draw_embeds(key, part):
    base = jax.random.fold_in(key, 505)
    key_one, key_two = jax.random.split(base, 2)
    columns = jnp.exp(jax.random.uniform(key_two, (MODEL_WIDTH,), jnp.float32, math.log(0.5), math.log(5.0)))
    values = jnp.clip(jax.random.normal(key_one, (TOKENS, MODEL_WIDTH), jnp.float32), -4.5, 4.5)
    return (values * columns[None, :]).astype(jnp.bfloat16)


def touch_ends(array, key, least, top_value):
    dims = array.shape
    place = [jax.random.randint(jax.random.fold_in(key, axis), (), 0, dims[axis]) for axis in range(len(dims))]
    array = array.at[tuple(place)].set(least)
    longest = dims.index(max(dims))
    place[longest] = (place[longest] + 1) % dims[longest]
    return array.at[tuple(place)].set(top_value)


def block_scale(stream_key, extent, pieces, low, top_value):
    def one(axis_at, blocks):
        heights = jax.random.uniform(jax.random.fold_in(jax.random.fold_in(stream_key, 6), axis_at), (blocks,), jnp.float32, low / len(pieces), top_value / len(pieces))
        return jnp.repeat(jnp.exp(heights), extent[axis_at] // blocks).reshape((-1,) + (1,) * (len(extent) - axis_at - 1))

    loudness = one(*pieces[0])
    for cut in pieces[1:]:
        loudness = loudness * one(*cut)
    return loudness


def centred(stream_key, extent, deviation, limit, cuts=(), dtype=jnp.bfloat16):
    entries = jax.random.normal(stream_key, extent, jnp.float32) * deviation
    if len(cuts) > 0:
        entries = block_scale(stream_key, extent, cuts, -0.22, 0.18) * entries
    return jnp.clip(entries, min=-limit, max=limit).astype(dtype)


def setup_inputs(seed: int = 0) -> dict:
    key_list = jax.random.split(jax.random.key(seed), 23)
    embeds = draw_embeds(jax.random.fold_in(key_list[22], 71), 0)
    input_norm_gain = jnp.clip(1.0 + 0.15 * jax.random.normal(key_list[1], (MODEL_WIDTH,), jnp.float32), 0.25, 1.75)
    input_norm_bias = centred(key_list[2], (MODEL_WIDTH,), 0.5, 3.0, (), jnp.float32)
    joined_projection_weight = centred(key_list[3], (MODEL_WIDTH, 3 * MODEL_WIDTH), MODEL_WIDTH ** -0.5, 0.125, ((1, 4),))
    joined_projection_bias = centred(key_list[4], (3 * MODEL_WIDTH,), 0.5, 3.0, ((0, 4),), jnp.float32)
    adapter_down_weight = centred(key_list[5], (TENANT_COUNT, MODEL_WIDTH, ADAPTER_RANK), MODEL_WIDTH ** -0.5, 0.125)
    adapter_up_weight = centred(key_list[6], (TENANT_COUNT, ADAPTER_RANK, 3 * MODEL_WIDTH), ADAPTER_RANK ** -0.5, 1.5, ((2, 4),))
    attention_out_weight = centred(key_list[7], (MODEL_WIDTH, MODEL_WIDTH), MODEL_WIDTH ** -0.5, 0.125, ((0, 4),))
    attention_out_bias = centred(key_list[8], (MODEL_WIDTH,), 0.5, 3.0, (), jnp.float32)
    post_attention_norm_gain = jnp.clip(jax.random.uniform(key_list[9], (MODEL_WIDTH,), jnp.float32, 0.4, 1.6), 0.4, 1.6)
    post_attention_norm_bias = centred(key_list[10], (MODEL_WIDTH,), 0.5, 3.0, (), jnp.float32)
    feedforward_up_weight = centred(key_list[11], (MODEL_WIDTH, FF), MODEL_WIDTH ** -0.5, 0.125, ((1, 4),))
    feedforward_up_bias = centred(key_list[12], (FF,), 0.5, 3.0, ((0, 4),), jnp.float32)
    feedforward_down_weight = centred(key_list[13], (FF, MODEL_WIDTH), FF ** -0.5, 0.09375, ((0, 4),))
    feedforward_down_bias = centred(key_list[14], (MODEL_WIDTH,), 0.5, 3.0, (), jnp.float32)
    stored_keys = draw_stored_keys(jax.random.fold_in(key_list[22], 71), 0)
    stored_values = centred(key_list[16], (REQS, CMAX, MODEL_WIDTH), 1.0, 6.0, ((0, 8), (2, 4)))
    stored_length = draw_stored_length(jax.random.fold_in(key_list[22], 71), 0)
    tenant_first_request = draw_tenant_first_request(jax.random.fold_in(key_list[22], 71), 0)
    accept = touch_ends((jax.random.randint(key_list[19], (TOKENS,), 0, 2) < 1).astype(jnp.int32), jax.random.fold_in(key_list[19], 1), 0, 1)
    replacement_token_index = draw_replacement_token_index(jax.random.fold_in(key_list[22], 71), 0)
    word_embedding_table = centred(key_list[21], (V, MODEL_WIDTH), 1.0, 6.0, ((0, 8), (1, 4)))
    return {"embeds": embeds, "input_norm_gain": input_norm_gain, "input_norm_bias": input_norm_bias, "joined_projection_weight": joined_projection_weight, "joined_projection_bias": joined_projection_bias, "adapter_down_weight": adapter_down_weight, "adapter_up_weight": adapter_up_weight, "attention_out_weight": attention_out_weight, "attention_out_bias": attention_out_bias, "post_attention_norm_gain": post_attention_norm_gain, "post_attention_norm_bias": post_attention_norm_bias, "feedforward_up_weight": feedforward_up_weight, "feedforward_up_bias": feedforward_up_bias, "feedforward_down_weight": feedforward_down_weight, "feedforward_down_bias": feedforward_down_bias, "stored_keys": stored_keys, "stored_values": stored_values, "stored_length": stored_length, "tenant_first_request": tenant_first_request, "accept": accept, "replacement_token_index": replacement_token_index, "word_embedding_table": word_embedding_table}


EPSILON = 1e-05

def layer_norm(residual_state, gain, shift):
    values = residual_state.astype(jnp.float32)
    row_mean = lax.optimization_barrier(jnp.mean(values, axis=-1, keepdims=True))
    centered = values - row_mean
    variance = lax.optimization_barrier(jnp.mean(centered * centered, axis=-1, keepdims=True))
    return (centered * lax.rsqrt(variance + EPSILON) * gain + shift).astype(jnp.bfloat16)

def attend_request(inputs):
    queries, keys_block, values_block, keys_cache, values_cache, length = inputs
    slopes = jnp.exp2(-8.0 * (jnp.arange(H) + 1).astype(jnp.float32) / H)
    block_pos = jnp.arange(BLK).astype(jnp.int32)
    cache_pos = jnp.arange(CMAX).astype(jnp.int32)
    keys_all = jnp.concatenate([keys_cache, keys_block], axis=0).astype(jnp.float32)
    values_all = jnp.concatenate([values_cache, values_block], axis=0).astype(jnp.float32)
    key_pos = jnp.concatenate([cache_pos, length + block_pos]).astype(jnp.int32)
    query_pos = (length + block_pos).astype(jnp.int32)
    scores = jnp.einsum('qhd,khd->hqk', queries.astype(jnp.float32), keys_all) / jnp.sqrt(jnp.float32(HD))
    distance = jnp.abs(query_pos[:, None] - key_pos[None, :]).astype(jnp.float32)
    scores = scores - slopes[:, None, None] * distance[None, :, :]
    valid = jnp.concatenate([cache_pos < length, block_pos >= 0])
    scores = jnp.where(valid[None, None, :], scores, -jnp.inf)
    row_max = lax.optimization_barrier(jnp.max(scores, axis=-1, keepdims=True))
    weights = jnp.exp(scores - row_max)
    summed = lax.optimization_barrier(jnp.sum(weights, axis=-1))
    rounded = lax.optimization_barrier(weights.astype(jnp.bfloat16))
    context = jnp.einsum('hqk,khd->qhd', rounded.astype(jnp.float32), values_all)
    context = context / jnp.transpose(summed)[:, :, None]
    return context.astype(jnp.bfloat16).reshape(BLK, H * HD)

def group_sum(left, right):
    group = left.shape[1] // N_TP
    summed = jnp.zeros((left.shape[0], right.shape[1]), jnp.float32)
    for index in range(N_TP):
        part = jnp.dot(left[:, index * group:(index + 1) * group], right[index * group:(index + 1) * group], preferred_element_type=jnp.float32).astype(jnp.bfloat16)
        summed = summed + lax.optimization_barrier(part).astype(jnp.float32)
    return summed

def run_layer_pass(residual_state, input_norm_gain, input_norm_bias, joined_projection_weight, joined_projection_bias, adapter_down_weight, adapter_up_weight, attention_out_weight, attention_out_bias, post_attention_norm_gain, post_attention_norm_bias, feedforward_up_weight, feedforward_up_bias, feedforward_down_weight, feedforward_down_bias, stored_keys, stored_values, stored_length, tenant_first_request):
    normed = layer_norm(residual_state, input_norm_gain, input_norm_bias)
    base = jnp.dot(normed, joined_projection_weight, preferred_element_type=jnp.float32)
    request_ids = jnp.arange(REQS).astype(jnp.int32)
    tenant_index = lax.optimization_barrier(jnp.sum((request_ids[:, None] >= tenant_first_request[None, :]).astype(jnp.int32), axis=1))
    tenant_grouped = normed.reshape(REQS, BLK, MODEL_WIDTH).astype(jnp.float32)
    low_rank_rows = jnp.einsum('evj,eji->evi', tenant_grouped, adapter_down_weight[tenant_index].astype(jnp.float32)).astype(jnp.bfloat16)
    low_rank_rows = lax.optimization_barrier(low_rank_rows)
    adapter_update = jnp.einsum('piw,pwl->pil', low_rank_rows.astype(jnp.float32), adapter_up_weight[tenant_index].astype(jnp.float32))
    joined = (base + adapter_update.reshape(TOKENS, 3 * MODEL_WIDTH) + joined_projection_bias).astype(jnp.bfloat16)
    parts = joined.reshape(REQS, BLK, H, 3, HD)
    context = lax.map(attend_request, (parts[:, :, :, 0], parts[:, :, :, 1], parts[:, :, :, 2], stored_keys.reshape(REQS, CMAX, H, HD), stored_values.reshape(REQS, CMAX, H, HD), stored_length))
    context = context.reshape(TOKENS, MODEL_WIDTH)
    attended = (residual_state.astype(jnp.float32) + group_sum(context, attention_out_weight) + attention_out_bias).astype(jnp.bfloat16)
    post = layer_norm(attended, post_attention_norm_gain, post_attention_norm_bias)
    hidden = jax.nn.gelu(jnp.dot(post, feedforward_up_weight, preferred_element_type=jnp.float32) + feedforward_up_bias, approximate=True).astype(jnp.bfloat16)
    return (attended.astype(jnp.float32) + group_sum(hidden, feedforward_down_weight) + feedforward_down_bias).astype(jnp.bfloat16)

def reference(embeds, input_norm_gain, input_norm_bias, joined_projection_weight, joined_projection_bias, adapter_down_weight, adapter_up_weight, attention_out_weight, attention_out_bias, post_attention_norm_gain, post_attention_norm_bias, feedforward_up_weight, feedforward_up_bias, feedforward_down_weight, feedforward_down_bias, stored_keys, stored_values, stored_length, tenant_first_request, accept, replacement_token_index, word_embedding_table):
    layer_parameters = (input_norm_gain, input_norm_bias, joined_projection_weight, joined_projection_bias, adapter_down_weight, adapter_up_weight, attention_out_weight, attention_out_bias, post_attention_norm_gain, post_attention_norm_bias, feedforward_up_weight, feedforward_up_bias, feedforward_down_weight, feedforward_down_bias, stored_keys, stored_values, stored_length, tenant_first_request)
    first = run_layer_pass(embeds, *layer_parameters)
    replaced = word_embedding_table[replacement_token_index]
    second_in = jnp.where((accept == 1)[:, None], replaced, first)
    return run_layer_pass(second_in, *layer_parameters)
```

```python
import functools

import jax
import jax.numpy as jnp
from jax import lax
from jax.experimental import pallas as pl
from jax.experimental.pallas import tpu as pltpu
from jax.sharding import PartitionSpec as P

H = 16
HD = 128
BLK = 256
EPSILON = 1e-05
F32 = jnp.float32
BF16 = jnp.bfloat16


def norm_rows(values, gain, shift):
    mean = jnp.mean(values, axis=-1, keepdims=True)
    centered = values - mean
    variance = jnp.mean(centered * centered, axis=-1, keepdims=True)
    return (centered * lax.rsqrt(variance + EPSILON) * gain + shift).astype(BF16)


def layer_kernel(
    n,
    rows,
    heads,
    length_ref,
    x_ref,
    in_gain,
    in_shift,
    wq_hbm,
    bq_ref,
    ad_ref,
    au_ref,
    wo_hbm,
    bo_ref,
    post_gain,
    post_shift,
    wu_hbm,
    bu_ref,
    wd_hbm,
    bd_ref,
    kc_hbm,
    vc_hbm,
    out_ref,
    wq,
    wo,
    wu,
    wd,
    kc,
    vc,
    gat_a,
    gat_b,
    part_a,
    part_b,
    from_left_a,
    from_right_a,
    from_left_b,
    from_right_b,
    qkv,
    ctx,
    hid,
    attended,
    load_sem,
    gat_send_right,
    gat_send_left,
    gat_recv,
    sum_send,
    sum_recv_left,
    sum_recv_right,
):
    me = lax.axis_index("tp")
    loads = [
        pltpu.make_async_copy(source, target, load_sem.at[index])
        for index, (source, target) in enumerate(
            ((wq_hbm, wq), (kc_hbm, kc), (vc_hbm, vc), (wo_hbm, wo), (wu_hbm, wu), (wd_hbm, wd))
        )
    ]
    for load in loads:
        load.start()
    has_left = me > 0
    has_right = me < n - 1

    barrier = pltpu.get_barrier_semaphore()

    @pl.when(has_left)
    def _():
        pl.semaphore_signal(
            barrier, inc=1, device_id={"tp": me - 1}, device_id_type=pl.DeviceIdType.MESH
        )

    @pl.when(has_right)
    def _():
        pl.semaphore_signal(
            barrier, inc=1, device_id={"tp": me + 1}, device_id_type=pl.DeviceIdType.MESH
        )

    def chunk(index):
        return pl.ds(pl.multiple_of(index * rows, rows), rows)

    gat_a[chunk(me), :] = norm_rows(x_ref[...].astype(F32), in_gain[...], in_shift[...])

    pl.semaphore_wait(barrier, has_left.astype(jnp.int32) + has_right.astype(jnp.int32))

    def gather_copy(which, buffer, index, step):
        sends = gat_send_right if step > 0 else gat_send_left
        return pltpu.make_async_remote_copy(
            src_ref=buffer.at[chunk(index), :],
            dst_ref=buffer.at[chunk(index), :],
            send_sem=sends.at[which, index],
            recv_sem=gat_recv.at[which, index],
            device_id={"tp": me + step},
            device_id_type=pl.DeviceIdType.MESH,
        )

    def gather(which, buffer):
        @pl.when(has_right)
        def _():
            gather_copy(which, buffer, me, 1).start()

        @pl.when(has_left)
        def _():
            gather_copy(which, buffer, me, -1).start()

        for k in range(1, n):

            @pl.when(me - k >= 0)
            def _():
                gather_copy(which, buffer, me - k, 1).wait_recv()

                @pl.when(has_right)
                def _():
                    gather_copy(which, buffer, me - k, 1).start()

            @pl.when(me + k <= n - 1)
            def _():
                gather_copy(which, buffer, me + k, -1).wait_recv()

                @pl.when(has_left)
                def _():
                    gather_copy(which, buffer, me + k, -1).start()

    def gather_end(which, buffer):
        for k in range(n):

            @pl.when((me - k >= 0) & has_right)
            def _():
                gather_copy(which, buffer, me - k, 1).wait_send()

            @pl.when((me + k <= n - 1) & has_left)
            def _():
                gather_copy(which, buffer, me + k, -1).wait_send()

    def sum_copy(which, part, landing, index, step):
        recvs = sum_recv_left if step > 0 else sum_recv_right
        return pltpu.make_async_remote_copy(
            src_ref=part.at[chunk(index), :],
            dst_ref=landing.at[chunk(index), :],
            send_sem=sum_send.at[which, index],
            recv_sem=recvs.at[which, index],
            device_id={"tp": me + step},
            device_id_type=pl.DeviceIdType.MESH,
        )

    def add_in(part, landing, index):
        part[chunk(index), :] = (
            part[chunk(index), :].astype(F32) + landing[chunk(index), :].astype(F32)
        ).astype(BF16)

    def sum_over(which, part, from_left, from_right):
        for k in range(n - 1):
            right_index = n - 1 - k
            left_index = k

            @pl.when(right_index > me)
            def _():
                @pl.when(has_left)
                def _():
                    sum_copy(which, part, from_left, right_index, 1).wait_recv()
                    add_in(part, from_left, right_index)

                sum_copy(which, part, from_left, right_index, 1).start()

            @pl.when(left_index < me)
            def _():
                @pl.when(has_right)
                def _():
                    sum_copy(which, part, from_right, left_index, -1).wait_recv()
                    add_in(part, from_right, left_index)

                sum_copy(which, part, from_right, left_index, -1).start()

        @pl.when(has_left)
        def _():
            sum_copy(which, part, from_left, me, 1).wait_recv()
            add_in(part, from_left, me)

        @pl.when(has_right)
        def _():
            sum_copy(which, part, from_right, me, -1).wait_recv()
            add_in(part, from_right, me)

    def sum_end(which, part, from_left, from_right):
        for k in range(n):

            @pl.when(k > me)
            def _():
                sum_copy(which, part, from_left, k, 1).wait_send()

            @pl.when(k < me)
            def _():
                sum_copy(which, part, from_right, k, -1).wait_send()

    def columns(index, width):
        return pl.ds(pl.multiple_of(index * width, width), width)

    gather(0, gat_a)
    loads[0].wait()
    low = jnp.dot(gat_a[...], ad_ref[...], preferred_element_type=F32).astype(BF16)

    @pl.loop(0, wq.shape[1] // 256)
    def _(tile):
        cols = columns(tile, 256)
        joined = jnp.dot(gat_a[...], wq[:, cols], preferred_element_type=F32)
        joined = joined + jnp.dot(low, au_ref[:, cols], preferred_element_type=F32)
        qkv[:, cols] = (joined + bq_ref[:, cols]).astype(BF16)

    loads[1].wait()
    loads[2].wait()
    length = length_ref[0]
    cache_rows = kc.shape[0]
    block = qkv.shape[0]
    scale = HD**-0.5

    @pl.loop(0, heads)
    def _(head):
        exponent = jnp.zeros((1, 1), F32) + (me * heads + head + 1).astype(F32) * (-8.0 / H)
        slope = jnp.exp2(exponent)
        query = qkv[:, columns(head * 3, HD)]
        key = qkv[:, columns(head * 3 + 1, HD)]
        value = qkv[:, columns(head * 3 + 2, HD)]
        contract = (((1,), (1,)), ((), ()))
        block_scores = lax.dot_general(query, key, contract, preferred_element_type=F32) * scale
        q_pos = lax.broadcasted_iota(jnp.int32, (block, 1), 0)
        k_pos = lax.broadcasted_iota(jnp.int32, (1, block), 1)
        block_scores = block_scores - slope * jnp.abs(q_pos - k_pos).astype(F32)
        cache_scores = (
            lax.dot_general(query, kc[:, columns(head, HD)], contract, preferred_element_type=F32)
            * scale
        )
        c_pos = lax.broadcasted_iota(jnp.int32, (1, cache_rows), 1)
        cache_scores = cache_scores - slope * (q_pos + length - c_pos).astype(F32)
        cache_scores = jnp.where(c_pos < length, cache_scores, -jnp.inf)
        top = jnp.maximum(
            jnp.max(block_scores, axis=-1, keepdims=True),
            jnp.max(cache_scores, axis=-1, keepdims=True),
        )
        block_weights = jnp.exp(block_scores - top)
        cache_weights = jnp.exp(cache_scores - top)
        total = jnp.sum(block_weights, axis=-1, keepdims=True) + jnp.sum(
            cache_weights, axis=-1, keepdims=True
        )
        mixed = jnp.dot(block_weights.astype(BF16), value, preferred_element_type=F32)
        mixed = mixed + jnp.dot(
            cache_weights.astype(BF16), vc[:, columns(head, HD)], preferred_element_type=F32
        )
        ctx[:, columns(head, HD)] = (mixed / total).astype(BF16)

    loads[3].wait()

    @pl.loop(0, wo.shape[1] // 256)
    def _(tile):
        cols = columns(tile, 256)
        part_a[:, cols] = jnp.dot(ctx[...], wo[:, cols], preferred_element_type=F32).astype(BF16)

    sum_over(0, part_a, from_left_a, from_right_a)
    attended[...] = (
        x_ref[...].astype(F32) + part_a[chunk(me), :].astype(F32) + bo_ref[...]
    ).astype(BF16)
    gat_b[chunk(me), :] = norm_rows(attended[...].astype(F32), post_gain[...], post_shift[...])
    gather(1, gat_b)
    loads[4].wait()

    @pl.loop(0, wu.shape[1] // 256)
    def _(tile):
        cols = columns(tile, 256)
        inner = jnp.dot(gat_b[...], wu[:, cols], preferred_element_type=F32) + bu_ref[:, cols]
        hid[:, cols] = jax.nn.gelu(inner, approximate=True).astype(BF16)

    loads[5].wait()

    @pl.loop(0, wd.shape[1] // 256)
    def _(tile):
        cols = columns(tile, 256)
        part_b[:, cols] = jnp.dot(hid[...], wd[:, cols], preferred_element_type=F32).astype(BF16)

    sum_over(1, part_b, from_left_b, from_right_b)
    out_ref[...] = (
        attended[...].astype(F32) + part_b[chunk(me), :].astype(F32) + bd_ref[...]
    ).astype(BF16)
    gather_end(0, gat_a)
    sum_end(0, part_a, from_left_a, from_right_a)
    gather_end(1, gat_b)
    sum_end(1, part_b, from_left_b, from_right_b)


def layer_call(n, x, length, weights):
    rows, width = x.shape
    wq, wo, wu, wd, kc, vc = weights[2], weights[6], weights[10], weights[12], weights[14], weights[15]
    heads = wo.shape[0] // HD
    block = n * rows
    vmem = pl.BlockSpec(memory_space=pltpu.VMEM)
    hbm = pl.BlockSpec(memory_space=pl.ANY)
    smem = pl.BlockSpec(memory_space=pltpu.SMEM)
    in_hbm = (2, 6, 10, 12, 14, 15)
    specs = [smem, vmem] + [hbm if i in in_hbm else vmem for i in range(len(weights))]
    full = pltpu.VMEM((block, width), BF16)
    dma = pltpu.SemaphoreType.DMA
    return pl.pallas_call(
        functools.partial(layer_kernel, n, rows, heads),
        out_shape=jax.ShapeDtypeStruct((rows, width), BF16),
        in_specs=specs,
        out_specs=vmem,
        scratch_shapes=[pltpu.VMEM(a.shape, BF16) for a in (wq, wo, wu, wd, kc, vc)]
        + [full] * 8
        + [
            pltpu.VMEM((block, wq.shape[1]), BF16),
            pltpu.VMEM((block, wo.shape[0]), BF16),
            pltpu.VMEM((block, wu.shape[1]), BF16),
            pltpu.VMEM((rows, width), BF16),
            dma((6,)),
        ]
        + [dma((2, n))] * 6,
        compiler_params=pltpu.CompilerParams(
            collective_id=0, has_side_effects=True, vmem_limit_bytes=52 * 2**20
        ),
        cost_estimate=pl.CostEstimate(
            flops=9_000_000_000, bytes_accessed=20_000_000, transcendentals=1_500_000
        ),
        name="layer_pass",
    )(length, x, *weights)


def shards(
    embeds,
    input_norm_gain,
    input_norm_bias,
    joined_projection_weight,
    joined_projection_bias,
    adapter_down_weight,
    adapter_up_weight,
    attention_out_weight,
    attention_out_bias,
    post_attention_norm_gain,
    post_attention_norm_bias,
    feedforward_up_weight,
    feedforward_up_bias,
    feedforward_down_weight,
    feedforward_down_bias,
    stored_keys,
    stored_values,
    stored_length,
    tenant_first_request,
    accept,
    replacement_token_index,
    word_embedding_table,
):
    n = lax.axis_size("tp")
    req_rank = lax.axis_index("req")
    table_rows = word_embedding_table.shape[0]
    tenant = jnp.sum((req_rank >= tenant_first_request).astype(jnp.int32))
    weights = (
        input_norm_gain[None],
        input_norm_bias[None],
        joined_projection_weight,
        joined_projection_bias[None],
        lax.dynamic_index_in_dim(adapter_down_weight, tenant, 0, keepdims=False),
        lax.dynamic_index_in_dim(adapter_up_weight, tenant, 0, keepdims=False),
        attention_out_weight,
        attention_out_bias[None],
        post_attention_norm_gain[None],
        post_attention_norm_bias[None],
        feedforward_up_weight,
        feedforward_up_bias[None],
        feedforward_down_weight,
        feedforward_down_bias[None],
        stored_keys[0],
        stored_values[0],
    )

    all_ids = lax.all_gather(replacement_token_index, "req", axis=0, tiled=True)
    local_index = all_ids - req_rank * table_rows
    inside = (local_index >= 0) & (local_index < table_rows)
    found = jnp.take(word_embedding_table, jnp.clip(local_index, 0, table_rows - 1), axis=0)
    found = jnp.where(inside[:, None], found.astype(F32), 0.0).astype(BF16)
    columns = lax.psum_scatter(found, "req", scatter_dimension=0, tiled=True)
    replacement = lax.all_to_all(columns, "tp", split_axis=0, concat_axis=1, tiled=True)
    first = layer_call(n, embeds, stored_length, weights)
    second_in = jnp.where((accept == 1)[:, None], replacement, first)
    return layer_call(n, second_in, stored_length, weights)


def solution(mesh):
    in_specs = (
        P(("req", "tp"), None),
        P(),
        P(),
        P(None, "tp"),
        P("tp"),
        P(),
        P(None, None, "tp"),
        P("tp", None),
        P(),
        P(),
        P(),
        P(None, "tp"),
        P("tp"),
        P("tp", None),
        P(),
        P("req", None, "tp"),
        P("req", None, "tp"),
        P("req"),
        P(),
        P(("req", "tp")),
        P("req"),
        P("req", "tp"),
    )
    out_specs = P(("req", "tp"), None)
    return jax.shard_map(shards, mesh=mesh, in_specs=in_specs, out_specs=out_specs, check_vma=False)
```

```python
import functools

import jax
import jax.numpy as jnp
from jax import lax
from jax.experimental import pallas as pl
from jax.experimental.pallas import tpu as pltpu
from jax.sharding import PartitionSpec as P

H = 16
HD = 128
BLK = 256
EPSILON = 1e-05
F32 = jnp.float32
BF16 = jnp.bfloat16


def norm_rows(values, gain, shift):
    mean = jnp.mean(values, axis=-1, keepdims=True)
    centered = values - mean
    variance = jnp.mean(centered * centered, axis=-1, keepdims=True)
    return (centered * lax.rsqrt(variance + EPSILON) * gain + shift).astype(BF16)


def layer_kernel(n, n_req, rows, heads, embed, *refs):
    refs = iter(refs)
    take = lambda count: [next(refs) for _ in range(count)]
    length_ref, x_ref, in_gain, in_shift, wq_hbm, bq_ref, ad_ref, au_ref = take(8)
    wo_hbm, bo_ref, post_gain, post_shift, wu_hbm, bu_ref, wd_hbm, bd_ref, kc_hbm, vc_hbm = take(10)
    if embed:
        found_ref, pick_ref, accept_ref = take(3)
    (out_ref,) = take(1)
    wq, wo, wu, wd, kc, vc = take(6)
    states, normed, post, attended, part_a, part_b = take(6)
    from_left_a, from_right_a, to_left, to_right, from_left_b, from_right_b = take(6)
    qkv, ctx, hid = take(3)
    load_sem, gat_send_right, gat_send_left, gat_recv = take(4)
    line_send_right, line_send_left, line_recv_left, line_recv_right = take(4)
    sum_send, sum_recv_left, sum_recv_right = take(3)
    if embed:
        landed, picked, replaced, row_send, row_recv, col_send, col_recv = take(7)
    mesh_id = pl.DeviceIdType.MESH
    me = lax.axis_index("tp")
    mine = lax.axis_index("req")
    loads = [
        pltpu.make_async_copy(source, target, load_sem.at[index])
        for index, (source, target) in enumerate(
            ((wq_hbm, wq), (kc_hbm, kc), (vc_hbm, vc), (wo_hbm, wo), (wu_hbm, wu), (wd_hbm, wd))
        )
    ]
    for load in loads:
        load.start()
    has_left = me > 0
    has_right = me < n - 1

    barrier = pltpu.get_barrier_semaphore()
    if embed:
        for k in range(1, n):
            pl.semaphore_signal(
                barrier, inc=1, device_id={"tp": lax.rem(me + k, n)}, device_id_type=mesh_id
            )
        for k in range(1, n_req):
            pl.semaphore_signal(
                barrier, inc=1, device_id={"req": lax.rem(mine + k, n_req)}, device_id_type=mesh_id
            )
    else:

        @pl.when(has_left)
        def _():
            pl.semaphore_signal(barrier, inc=1, device_id={"tp": me - 1}, device_id_type=mesh_id)

        @pl.when(has_right)
        def _():
            pl.semaphore_signal(barrier, inc=1, device_id={"tp": me + 1}, device_id_type=mesh_id)

    def chunk(index):
        return pl.ds(pl.multiple_of(index * rows, rows), rows)

    def zero(buffer):
        buffer[...] = jnp.zeros(buffer.shape, buffer.dtype)

    states[chunk(me), :] = x_ref[...]

    @pl.when(jnp.logical_not(has_left))
    def _():
        zero(from_left_a)

    @pl.when(jnp.logical_not(has_right))
    def _():
        zero(from_right_a)

    if embed:
        pl.semaphore_wait(barrier, n - 1 + n_req - 1)
    else:
        pl.semaphore_wait(barrier, has_left.astype(jnp.int32) + has_right.astype(jnp.int32))

    def gather_copy(index, step):
        sends = gat_send_right if step > 0 else gat_send_left
        return pltpu.make_async_remote_copy(
            src_ref=states.at[chunk(index), :],
            dst_ref=states.at[chunk(index), :],
            send_sem=sends.at[index],
            recv_sem=gat_recv.at[index],
            device_id={"tp": me + step},
            device_id_type=mesh_id,
        )

    def norm_in(index):
        normed[chunk(index), :] = norm_rows(
            states[chunk(index), :].astype(F32), in_gain[...], in_shift[...]
        )

    @pl.when(has_right)
    def _():
        gather_copy(me, 1).start()

    @pl.when(has_left)
    def _():
        gather_copy(me, -1).start()

    if embed:
        cap = found_ref.shape[0] // n_req

        def row_block(index):
            return pl.ds(pl.multiple_of(index * cap, cap), cap)

        def row_copy(peer, source):
            return pltpu.make_async_remote_copy(
                src_ref=found_ref.at[row_block(peer), :],
                dst_ref=landed.at[row_block(source), :],
                send_sem=row_send.at[peer],
                recv_sem=row_recv.at[source],
                device_id={"req": peer},
                device_id_type=mesh_id,
            )

        for k in range(1, n_req):
            row_copy(lax.rem(mine + k, n_req), mine).start()
        landed[row_block(mine), :] = found_ref[row_block(mine), :]

    norm_in(me)
    for k in range(1, n):

        @pl.when(me - k >= 0)
        def _():
            gather_copy(me - k, 1).wait_recv()

            @pl.when(has_right)
            def _():
                gather_copy(me - k, 1).start()

        @pl.when(me + k <= n - 1)
        def _():
            gather_copy(me + k, -1).wait_recv()

            @pl.when(has_left)
            def _():
                gather_copy(me + k, -1).start()

        @pl.when(me - k >= 0)
        def _():
            norm_in(me - k)

        @pl.when(me + k <= n - 1)
        def _():
            norm_in(me + k)

    def columns(index, width):
        return pl.ds(pl.multiple_of(index * width, width), width)

    loads[0].wait()
    low = jnp.dot(normed[...], ad_ref[...], preferred_element_type=F32).astype(BF16)

    @pl.loop(0, wq.shape[1] // 256)
    def _(tile):
        cols = columns(tile, 256)
        joined = jnp.dot(normed[...], wq[:, cols], preferred_element_type=F32)
        joined = joined + jnp.dot(low, au_ref[:, cols], preferred_element_type=F32)
        qkv[:, cols] = (joined + bq_ref[:, cols]).astype(BF16)

    if embed:
        for k in range(1, n_req):
            peer = lax.rem(mine + k, n_req)
            row_copy(peer, peer).wait_recv()
        slots = lax.broadcasted_iota(jnp.int32, (pick_ref.shape[0], landed.shape[0]), 1)
        chosen = jnp.where(slots == pick_ref[...], 1.0, 0.0).astype(BF16)
        picked[...] = jnp.dot(chosen, landed[...], preferred_element_type=F32).astype(BF16)

        def column_copy(peer, source):
            return pltpu.make_async_remote_copy(
                src_ref=picked.at[chunk(peer), :],
                dst_ref=replaced.at[source],
                send_sem=col_send.at[peer],
                recv_sem=col_recv.at[source],
                device_id={"tp": peer},
                device_id_type=mesh_id,
            )

        for k in range(1, n):
            column_copy(lax.rem(me + k, n), me).start()
        replaced[me] = picked[chunk(me), :]

    loads[1].wait()
    loads[2].wait()
    length = length_ref[0]
    cache_rows = kc.shape[0]
    block = qkv.shape[0]
    scale = HD**-0.5

    @pl.loop(0, heads)
    def _(head):
        exponent = jnp.zeros((1, 1), F32) + (me * heads + head + 1).astype(F32) * (-8.0 / H)
        slope = jnp.exp2(exponent)
        query = qkv[:, columns(head * 3, HD)]
        key = qkv[:, columns(head * 3 + 1, HD)]
        value = qkv[:, columns(head * 3 + 2, HD)]
        contract = (((1,), (1,)), ((), ()))
        block_scores = lax.dot_general(query, key, contract, preferred_element_type=F32) * scale
        q_pos = lax.broadcasted_iota(jnp.int32, (block, 1), 0)
        k_pos = lax.broadcasted_iota(jnp.int32, (1, block), 1)
        block_scores = block_scores - slope * jnp.abs(q_pos - k_pos).astype(F32)
        cache_scores = (
            lax.dot_general(query, kc[:, columns(head, HD)], contract, preferred_element_type=F32)
            * scale
        )
        c_pos = lax.broadcasted_iota(jnp.int32, (1, cache_rows), 1)
        cache_scores = cache_scores - slope * (q_pos + length - c_pos).astype(F32)
        cache_scores = jnp.where(c_pos < length, cache_scores, -jnp.inf)
        top = jnp.maximum(
            jnp.max(block_scores, axis=-1, keepdims=True),
            jnp.max(cache_scores, axis=-1, keepdims=True),
        )
        block_weights = jnp.exp(block_scores - top)
        cache_weights = jnp.exp(cache_scores - top)
        total = jnp.sum(block_weights, axis=-1, keepdims=True) + jnp.sum(
            cache_weights, axis=-1, keepdims=True
        )
        mixed = jnp.dot(block_weights.astype(BF16), value, preferred_element_type=F32)
        mixed = mixed + jnp.dot(
            cache_weights.astype(BF16), vc[:, columns(head, HD)], preferred_element_type=F32
        )
        ctx[:, columns(head, HD)] = (mixed / total).astype(BF16)

    loads[3].wait()

    @pl.loop(0, wo.shape[1] // 256)
    def _(tile):
        cols = columns(tile, 256)
        part_a[:, cols] = jnp.dot(ctx[...], wo[:, cols], preferred_element_type=F32).astype(BF16)

    piece_rows = 16
    pieces = block // piece_rows

    def piece(index):
        return pl.ds(pl.multiple_of(index * piece_rows, piece_rows), piece_rows)

    def line_right(index):
        return pltpu.make_async_remote_copy(
            src_ref=to_right.at[piece(index), :],
            dst_ref=from_left_a.at[piece(index), :],
            send_sem=line_send_right.at[index],
            recv_sem=line_recv_left.at[index],
            device_id={"tp": me + 1},
            device_id_type=mesh_id,
        )

    def line_left(index):
        return pltpu.make_async_remote_copy(
            src_ref=to_left.at[piece(index), :],
            dst_ref=from_right_a.at[piece(index), :],
            send_sem=line_send_left.at[index],
            recv_sem=line_recv_right.at[index],
            device_id={"tp": me - 1},
            device_id_type=mesh_id,
        )

    @pl.loop(0, pieces + n - 1)
    def _(step):
        right_piece = step - me
        left_piece = step - (n - 1 - me)
        done_piece = step - (n - 1)

        @pl.when((right_piece >= 0) & (right_piece < pieces))
        def _():
            @pl.when(has_left)
            def _():
                line_right(right_piece).wait_recv()

            @pl.when(has_right)
            def _():
                here = piece(right_piece)
                to_right[here, :] = (
                    part_a[here, :].astype(F32) + from_left_a[here, :].astype(F32)
                ).astype(BF16)
                line_right(right_piece).start()

        @pl.when((left_piece >= 0) & (left_piece < pieces))
        def _():
            @pl.when(has_right)
            def _():
                line_left(left_piece).wait_recv()

            @pl.when(has_left)
            def _():
                here = piece(left_piece)
                to_left[here, :] = (
                    part_a[here, :].astype(F32) + from_right_a[here, :].astype(F32)
                ).astype(BF16)
                line_left(left_piece).start()

        @pl.when(done_piece >= 0)
        def _():
            here = piece(done_piece)
            summed = part_a[here, :].astype(F32) + from_left_a[here, :].astype(F32)
            summed = summed + from_right_a[here, :].astype(F32)
            summed = (states[here, :].astype(F32) + summed + bo_ref[...]).astype(BF16)
            attended[here, :] = summed
            post[here, :] = norm_rows(summed.astype(F32), post_gain[...], post_shift[...])

    loads[4].wait()

    @pl.loop(0, wu.shape[1] // 256)
    def _(tile):
        cols = columns(tile, 256)
        inner = jnp.dot(post[...], wu[:, cols], preferred_element_type=F32) + bu_ref[:, cols]
        hid[:, cols] = jax.nn.gelu(inner, approximate=True).astype(BF16)

    loads[5].wait()

    @pl.loop(0, wd.shape[1] // 256)
    def _(tile):
        cols = columns(tile, 256)
        part_b[:, cols] = jnp.dot(hid[...], wd[:, cols], preferred_element_type=F32).astype(BF16)

    def sum_copy(landing, index, step):
        recvs = sum_recv_left if step > 0 else sum_recv_right
        return pltpu.make_async_remote_copy(
            src_ref=part_b.at[chunk(index), :],
            dst_ref=landing.at[chunk(index), :],
            send_sem=sum_send.at[index],
            recv_sem=recvs.at[index],
            device_id={"tp": me + step},
            device_id_type=mesh_id,
        )

    def add_in(landing, index):
        part_b[chunk(index), :] = (
            part_b[chunk(index), :].astype(F32) + landing[chunk(index), :].astype(F32)
        ).astype(BF16)

    for k in range(n - 1):
        right_index = n - 1 - k
        left_index = k

        @pl.when(right_index > me)
        def _():
            @pl.when(has_left)
            def _():
                sum_copy(from_left_b, right_index, 1).wait_recv()
                add_in(from_left_b, right_index)

            sum_copy(from_left_b, right_index, 1).start()

        @pl.when(left_index < me)
        def _():
            @pl.when(has_right)
            def _():
                sum_copy(from_right_b, left_index, -1).wait_recv()
                add_in(from_right_b, left_index)

            sum_copy(from_right_b, left_index, -1).start()

    @pl.when(has_left)
    def _():
        sum_copy(from_left_b, me, 1).wait_recv()
        add_in(from_left_b, me)

    @pl.when(has_right)
    def _():
        sum_copy(from_right_b, me, -1).wait_recv()
        add_in(from_right_b, me)

    result = (
        attended[chunk(me), :].astype(F32) + part_b[chunk(me), :].astype(F32) + bd_ref[...]
    ).astype(BF16)
    if embed:
        width = replaced.shape[2]
        for k in range(1, n):
            peer = lax.rem(me + k, n)
            column_copy(peer, peer).wait_recv()
        for k in range(n):
            cols = slice(k * width, (k + 1) * width)
            out_ref[:, cols] = jnp.where(accept_ref[...] == 1, replaced[k], result[:, cols])
        for k in range(1, n):
            column_copy(lax.rem(me + k, n), me).wait_send()
        for k in range(1, n_req):
            row_copy(lax.rem(mine + k, n_req), mine).wait_send()
    else:
        out_ref[...] = result

    for k in range(n):

        @pl.when((me - k >= 0) & has_right)
        def _():
            gather_copy(me - k, 1).wait_send()

        @pl.when((me + k <= n - 1) & has_left)
        def _():
            gather_copy(me + k, -1).wait_send()

        @pl.when(k > me)
        def _():
            sum_copy(from_left_b, k, 1).wait_send()

        @pl.when(k < me)
        def _():
            sum_copy(from_right_b, k, -1).wait_send()

    @pl.loop(0, pieces)
    def _(index):
        @pl.when(has_right)
        def _():
            line_right(index).wait_send()

        @pl.when(has_left)
        def _():
            line_left(index).wait_send()


def layer_call(n, n_req, x, length, weights, extra):
    rows, width = x.shape
    wq, wo, wu, wd, kc, vc = weights[2], weights[6], weights[10], weights[12], weights[14], weights[15]
    heads = wo.shape[0] // HD
    block = n * rows
    embed = len(extra) > 0
    vmem = pl.BlockSpec(memory_space=pltpu.VMEM)
    hbm = pl.BlockSpec(memory_space=pl.ANY)
    smem = pl.BlockSpec(memory_space=pltpu.SMEM)
    in_hbm = (2, 6, 10, 12, 14, 15)
    specs = [smem, vmem] + [hbm if i in in_hbm else vmem for i in range(len(weights))]
    specs = specs + [vmem] * len(extra)
    full = pltpu.VMEM((block, width), BF16)
    dma = pltpu.SemaphoreType.DMA
    scratch = [pltpu.VMEM(a.shape, BF16) for a in (wq, wo, wu, wd, kc, vc)] + [full] * 12
    scratch = scratch + [
        pltpu.VMEM((block, wq.shape[1]), BF16),
        pltpu.VMEM((block, wo.shape[0]), BF16),
        pltpu.VMEM((block, wu.shape[1]), BF16),
        dma((6,)),
    ]
    scratch = scratch + [dma((n,))] * 3 + [dma((block // 16,))] * 4 + [dma((n,))] * 3
    if embed:
        part = extra[0].shape[1]
        scratch = scratch + [
            pltpu.VMEM(extra[0].shape, BF16),
            pltpu.VMEM((block, part), BF16),
            pltpu.VMEM((n, rows, part), BF16),
            dma((n_req,)),
            dma((n_req,)),
            dma((n,)),
            dma((n,)),
        ]
    return pl.pallas_call(
        functools.partial(layer_kernel, n, n_req, rows, heads, embed),
        out_shape=jax.ShapeDtypeStruct((rows, width), BF16),
        in_specs=specs,
        out_specs=vmem,
        scratch_shapes=scratch,
        compiler_params=pltpu.CompilerParams(
            collective_id=1 if embed else 0,
            has_side_effects=True,
            vmem_limit_bytes=54 * 2**20,
        ),
        cost_estimate=pl.CostEstimate(
            flops=9_000_000_000, bytes_accessed=20_000_000, transcendentals=1_500_000
        ),
        name="first_pass" if embed else "second_pass",
    )(length, x, *weights, *extra)


def shards(
    embeds,
    input_norm_gain,
    input_norm_bias,
    joined_projection_weight,
    joined_projection_bias,
    adapter_down_weight,
    adapter_up_weight,
    attention_out_weight,
    attention_out_bias,
    post_attention_norm_gain,
    post_attention_norm_bias,
    feedforward_up_weight,
    feedforward_up_bias,
    feedforward_down_weight,
    feedforward_down_bias,
    stored_keys,
    stored_values,
    stored_length,
    tenant_first_request,
    accept,
    replacement_token_index,
    word_embedding_table,
):
    n = lax.axis_size("tp")
    req_rank = lax.axis_index("req")
    table_rows = word_embedding_table.shape[0]
    tenant = jnp.sum((req_rank >= tenant_first_request).astype(jnp.int32))
    weights = (
        input_norm_gain[None],
        input_norm_bias[None],
        joined_projection_weight,
        joined_projection_bias[None],
        lax.dynamic_index_in_dim(adapter_down_weight, tenant, 0, keepdims=False),
        lax.dynamic_index_in_dim(adapter_up_weight, tenant, 0, keepdims=False),
        attention_out_weight,
        attention_out_bias[None],
        post_attention_norm_gain[None],
        post_attention_norm_bias[None],
        feedforward_up_weight,
        feedforward_up_bias[None],
        feedforward_down_weight,
        feedforward_down_bias[None],
        stored_keys[0],
        stored_values[0],
    )

    n_req = lax.axis_size("req")
    block = replacement_token_index.shape[0]
    cap = (3 * block // n_req + 15) // 16 * 16
    owner = replacement_token_index // table_rows
    place = jnp.arange(block)
    earlier = (owner[:, None] == owner[None, :]) & (place[None, :] < place[:, None])
    rank = jnp.sum(earlier.astype(jnp.int32), axis=1)
    pick = (owner * cap + rank)[:, None]

    all_ids = lax.all_gather(replacement_token_index, "req", axis=0)
    local_index = all_ids - req_rank * table_rows
    inside = (local_index >= 0) & (local_index < table_rows)
    before = (place[:, None] < place[None, :]).astype(BF16)
    slot = jnp.dot(inside.astype(BF16), before, preferred_element_type=F32).astype(jnp.int32)
    slot = jnp.where(inside, slot, -1)
    hit = slot[:, None, :] == jnp.arange(cap)[None, :, None]
    wanted = jnp.sum(jnp.where(hit, local_index[:, None, :], 0), axis=2).reshape(-1)
    found = word_embedding_table.at[wanted].get(mode="promise_in_bounds")
    extra = (found, pick, accept[:, None])
    second_in = layer_call(n, n_req, embeds, stored_length, weights, extra)
    return layer_call(n, n_req, second_in, stored_length, weights, ())


def solution(mesh):
    in_specs = (
        P(("req", "tp"), None),
        P(),
        P(),
        P(None, "tp"),
        P("tp"),
        P(),
        P(None, None, "tp"),
        P("tp", None),
        P(),
        P(),
        P(),
        P(None, "tp"),
        P("tp"),
        P("tp", None),
        P(),
        P("req", None, "tp"),
        P("req", None, "tp"),
        P("req"),
        P(),
        P(("req", "tp")),
        P("req"),
        P("req", "tp"),
    )
    out_specs = P(("req", "tp"), None)
    return jax.shard_map(shards, mesh=mesh, in_specs=in_specs, out_specs=out_specs, check_vma=False)
```

```python
import functools

import jax
import jax.numpy as jnp
from jax import lax
from jax.experimental import pallas as pl
from jax.experimental.pallas import tpu as pltpu
from jax.sharding import PartitionSpec as P

H = 16
HD = 128
BLK = 256
EPSILON = 1e-05
F32 = jnp.float32
BF16 = jnp.bfloat16


def norm_rows(values, gain, shift):
    mean = jnp.mean(values, axis=-1, keepdims=True)
    centered = values - mean
    variance = jnp.mean(centered * centered, axis=-1, keepdims=True)
    return (centered * lax.rsqrt(variance + EPSILON) * gain + shift).astype(BF16)


def layer_kernel(n, n_req, rows, heads, embed, *refs):
    refs = iter(refs)
    take = lambda count: [next(refs) for _ in range(count)]
    length_ref, x_ref, in_gain, in_shift, wq_hbm, bq_ref, ad_ref, au_ref = take(8)
    wo_hbm, bo_ref, post_gain, post_shift, wu_hbm, bu_ref, wd_hbm, bd_ref, kc_hbm, vc_hbm = take(10)
    if embed:
        found_ref, pick_ref, accept_ref = take(3)
    (out_ref,) = take(1)
    wq, wo, wu, wd, kc, vc = take(6)
    states, normed, post, attended, part_a, part_b = take(6)
    from_left_a, from_right_a, to_left, to_right, from_left_b, from_right_b = take(6)
    qkv, ctx, hid = take(3)
    load_sem, gat_send_right, gat_send_left, gat_recv = take(4)
    line_send_right, line_send_left, line_recv_left, line_recv_right = take(4)
    sum_send, sum_recv_left, sum_recv_right = take(3)
    if embed:
        landed, picked, replaced, row_send, row_recv, col_send, col_recv = take(7)
    mesh_id = pl.DeviceIdType.MESH
    me = lax.axis_index("tp")
    mine = lax.axis_index("req")
    loads = [
        pltpu.make_async_copy(source, target, load_sem.at[index])
        for index, (source, target) in enumerate(
            ((wq_hbm, wq), (kc_hbm, kc), (vc_hbm, vc), (wo_hbm, wo), (wu_hbm, wu), (wd_hbm, wd))
        )
    ]
    for load in loads:
        load.start()
    has_left = me > 0
    has_right = me < n - 1

    barrier = pltpu.get_barrier_semaphore()
    if embed:
        for k in range(1, n):
            pl.semaphore_signal(
                barrier, inc=1, device_id={"tp": lax.rem(me + k, n)}, device_id_type=mesh_id
            )
        for k in range(1, n_req):
            pl.semaphore_signal(
                barrier, inc=1, device_id={"req": lax.rem(mine + k, n_req)}, device_id_type=mesh_id
            )
    else:

        @pl.when(has_left)
        def _():
            pl.semaphore_signal(barrier, inc=1, device_id={"tp": me - 1}, device_id_type=mesh_id)

        @pl.when(has_right)
        def _():
            pl.semaphore_signal(barrier, inc=1, device_id={"tp": me + 1}, device_id_type=mesh_id)

    def chunk(index):
        return pl.ds(pl.multiple_of(index * rows, rows), rows)

    def zero(buffer):
        buffer[...] = jnp.zeros(buffer.shape, buffer.dtype)

    states[chunk(me), :] = x_ref[...]

    @pl.when(jnp.logical_not(has_left))
    def _():
        zero(from_left_a)

    @pl.when(jnp.logical_not(has_right))
    def _():
        zero(from_right_a)

    if embed:
        pl.semaphore_wait(barrier, n - 1 + n_req - 1)
    else:
        pl.semaphore_wait(barrier, has_left.astype(jnp.int32) + has_right.astype(jnp.int32))

    def gather_copy(index, step):
        sends = gat_send_right if step > 0 else gat_send_left
        return pltpu.make_async_remote_copy(
            src_ref=states.at[chunk(index), :],
            dst_ref=states.at[chunk(index), :],
            send_sem=sends.at[index],
            recv_sem=gat_recv.at[index],
            device_id={"tp": me + step},
            device_id_type=mesh_id,
        )

    def norm_in(index):
        normed[chunk(index), :] = norm_rows(
            states[chunk(index), :].astype(F32), in_gain[...], in_shift[...]
        )

    @pl.when(has_right)
    def _():
        gather_copy(me, 1).start()

    @pl.when(has_left)
    def _():
        gather_copy(me, -1).start()

    if embed:
        cap = found_ref.shape[0] // n_req

        def row_block(index):
            return pl.ds(pl.multiple_of(index * cap, cap), cap)

        def row_copy(peer, source):
            return pltpu.make_async_remote_copy(
                src_ref=found_ref.at[row_block(peer), :],
                dst_ref=landed.at[row_block(source), :],
                send_sem=row_send.at[peer],
                recv_sem=row_recv.at[source],
                device_id={"req": peer},
                device_id_type=mesh_id,
            )

        for k in range(1, n_req):
            row_copy(lax.rem(mine + k, n_req), mine).start()
        landed[row_block(mine), :] = found_ref[row_block(mine), :]

    norm_in(me)
    for k in range(1, n):

        @pl.when(me - k >= 0)
        def _():
            gather_copy(me - k, 1).wait_recv()

            @pl.when(has_right)
            def _():
                gather_copy(me - k, 1).start()

        @pl.when(me + k <= n - 1)
        def _():
            gather_copy(me + k, -1).wait_recv()

            @pl.when(has_left)
            def _():
                gather_copy(me + k, -1).start()

        @pl.when(me - k >= 0)
        def _():
            norm_in(me - k)

        @pl.when(me + k <= n - 1)
        def _():
            norm_in(me + k)

    def columns(index, width):
        return pl.ds(pl.multiple_of(index * width, width), width)

    loads[0].wait()
    low = jnp.dot(normed[...], ad_ref[...], preferred_element_type=F32).astype(BF16)

    @pl.loop(0, wq.shape[1] // 256)
    def _(tile):
        cols = columns(tile, 256)
        joined = jnp.dot(normed[...], wq[:, cols], preferred_element_type=F32)
        joined = joined + jnp.dot(low, au_ref[:, cols], preferred_element_type=F32)
        qkv[:, cols] = (joined + bq_ref[:, cols]).astype(BF16)

    if embed:
        for k in range(1, n_req):
            peer = lax.rem(mine + k, n_req)
            row_copy(peer, peer).wait_recv()
        slots = lax.broadcasted_iota(jnp.int32, (pick_ref.shape[0], landed.shape[0]), 1)
        chosen = jnp.where(slots == pick_ref[...], 1.0, 0.0).astype(BF16)
        picked[...] = jnp.dot(chosen, landed[...], preferred_element_type=F32).astype(BF16)

        def column_copy(peer, source):
            return pltpu.make_async_remote_copy(
                src_ref=picked.at[chunk(peer), :],
                dst_ref=replaced.at[source],
                send_sem=col_send.at[peer],
                recv_sem=col_recv.at[source],
                device_id={"tp": peer},
                device_id_type=mesh_id,
            )

        for k in range(1, n):
            column_copy(lax.rem(me + k, n), me).start()
        replaced[me] = picked[chunk(me), :]

    loads[1].wait()
    loads[2].wait()
    length = length_ref[0]
    cache_rows = kc.shape[0]
    block = qkv.shape[0]
    scale = HD**-0.5

    @pl.loop(0, heads)
    def _(head):
        exponent = jnp.zeros((1, 1), F32) + (me * heads + head + 1).astype(F32) * (-8.0 / H)
        slope = jnp.exp2(exponent)
        query = qkv[:, columns(head * 3, HD)]
        key = qkv[:, columns(head * 3 + 1, HD)]
        value = qkv[:, columns(head * 3 + 2, HD)]
        contract = (((1,), (1,)), ((), ()))
        block_scores = lax.dot_general(query, key, contract, preferred_element_type=F32) * scale
        q_pos = lax.broadcasted_iota(jnp.int32, (block, 1), 0)
        k_pos = lax.broadcasted_iota(jnp.int32, (1, block), 1)
        block_scores = block_scores - slope * jnp.abs(q_pos - k_pos).astype(F32)
        cache_scores = (
            lax.dot_general(query, kc[:, columns(head, HD)], contract, preferred_element_type=F32)
            * scale
        )
        c_pos = lax.broadcasted_iota(jnp.int32, (1, cache_rows), 1)
        cache_scores = cache_scores - slope * (q_pos + length - c_pos).astype(F32)
        cache_scores = jnp.where(c_pos < length, cache_scores, -jnp.inf)
        top = jnp.maximum(
            jnp.max(block_scores, axis=-1, keepdims=True),
            jnp.max(cache_scores, axis=-1, keepdims=True),
        )
        block_weights = jnp.exp(block_scores - top)
        cache_weights = jnp.exp(cache_scores - top)
        total = jnp.sum(block_weights, axis=-1, keepdims=True) + jnp.sum(
            cache_weights, axis=-1, keepdims=True
        )
        mixed = jnp.dot(block_weights.astype(BF16), value, preferred_element_type=F32)
        mixed = mixed + jnp.dot(
            cache_weights.astype(BF16), vc[:, columns(head, HD)], preferred_element_type=F32
        )
        ctx[:, columns(head, HD)] = (mixed / total).astype(BF16)

    loads[3].wait()

    @pl.loop(0, wo.shape[1] // 256)
    def _(tile):
        cols = columns(tile, 256)
        part_a[:, cols] = jnp.dot(ctx[...], wo[:, cols], preferred_element_type=F32).astype(BF16)

    piece_rows = 16
    lag = 5
    pieces = block // piece_rows

    def piece(index):
        return pl.ds(pl.multiple_of(index * piece_rows, piece_rows), piece_rows)

    def line_right(index):
        return pltpu.make_async_remote_copy(
            src_ref=to_right.at[piece(index), :],
            dst_ref=from_left_a.at[piece(index), :],
            send_sem=line_send_right.at[index],
            recv_sem=line_recv_left.at[index],
            device_id={"tp": me + 1},
            device_id_type=mesh_id,
        )

    def line_left(index):
        return pltpu.make_async_remote_copy(
            src_ref=to_left.at[piece(index), :],
            dst_ref=from_right_a.at[piece(index), :],
            send_sem=line_send_left.at[index],
            recv_sem=line_recv_right.at[index],
            device_id={"tp": me - 1},
            device_id_type=mesh_id,
        )

    @pl.loop(0, pieces + lag * (n - 1))
    def _(step):
        right_piece = step - lag * me
        left_piece = step - lag * (n - 1 - me)
        done_piece = step - lag * (n - 1)

        @pl.when((right_piece >= 0) & (right_piece < pieces))
        def _():
            @pl.when(has_left)
            def _():
                line_right(right_piece).wait_recv()

            @pl.when(has_right)
            def _():
                here = piece(right_piece)
                to_right[here, :] = (
                    part_a[here, :].astype(F32) + from_left_a[here, :].astype(F32)
                ).astype(BF16)
                line_right(right_piece).start()

        @pl.when((left_piece >= 0) & (left_piece < pieces))
        def _():
            @pl.when(has_right)
            def _():
                line_left(left_piece).wait_recv()

            @pl.when(has_left)
            def _():
                here = piece(left_piece)
                to_left[here, :] = (
                    part_a[here, :].astype(F32) + from_right_a[here, :].astype(F32)
                ).astype(BF16)
                line_left(left_piece).start()

        @pl.when(done_piece >= 0)
        def _():
            here = piece(done_piece)
            summed = part_a[here, :].astype(F32) + from_left_a[here, :].astype(F32)
            summed = summed + from_right_a[here, :].astype(F32)
            summed = (states[here, :].astype(F32) + summed + bo_ref[...]).astype(BF16)
            attended[here, :] = summed
            post[here, :] = norm_rows(summed.astype(F32), post_gain[...], post_shift[...])

    loads[4].wait()

    @pl.loop(0, wu.shape[1] // 256)
    def _(tile):
        cols = columns(tile, 256)
        inner = jnp.dot(post[...], wu[:, cols], preferred_element_type=F32) + bu_ref[:, cols]
        hid[:, cols] = jax.nn.gelu(inner, approximate=True).astype(BF16)

    loads[5].wait()

    @pl.loop(0, wd.shape[1] // 256)
    def _(tile):
        cols = columns(tile, 256)
        part_b[:, cols] = jnp.dot(hid[...], wd[:, cols], preferred_element_type=F32).astype(BF16)

    def sum_copy(landing, index, step):
        recvs = sum_recv_left if step > 0 else sum_recv_right
        return pltpu.make_async_remote_copy(
            src_ref=part_b.at[chunk(index), :],
            dst_ref=landing.at[chunk(index), :],
            send_sem=sum_send.at[index],
            recv_sem=recvs.at[index],
            device_id={"tp": me + step},
            device_id_type=mesh_id,
        )

    def add_in(landing, index):
        part_b[chunk(index), :] = (
            part_b[chunk(index), :].astype(F32) + landing[chunk(index), :].astype(F32)
        ).astype(BF16)

    for k in range(n - 1):
        right_index = n - 1 - k
        left_index = k

        @pl.when(right_index > me)
        def _():
            @pl.when(has_left)
            def _():
                sum_copy(from_left_b, right_index, 1).wait_recv()
                add_in(from_left_b, right_index)

            sum_copy(from_left_b, right_index, 1).start()

        @pl.when(left_index < me)
        def _():
            @pl.when(has_right)
            def _():
                sum_copy(from_right_b, left_index, -1).wait_recv()
                add_in(from_right_b, left_index)

            sum_copy(from_right_b, left_index, -1).start()

    @pl.when(has_left)
    def _():
        sum_copy(from_left_b, me, 1).wait_recv()
        add_in(from_left_b, me)

    @pl.when(has_right)
    def _():
        sum_copy(from_right_b, me, -1).wait_recv()
        add_in(from_right_b, me)

    result = (
        attended[chunk(me), :].astype(F32) + part_b[chunk(me), :].astype(F32) + bd_ref[...]
    ).astype(BF16)
    if embed:
        width = replaced.shape[2]
        for k in range(1, n):
            peer = lax.rem(me + k, n)
            column_copy(peer, peer).wait_recv()
        for k in range(n):
            cols = slice(k * width, (k + 1) * width)
            out_ref[:, cols] = jnp.where(accept_ref[...] == 1, replaced[k], result[:, cols])
        for k in range(1, n):
            column_copy(lax.rem(me + k, n), me).wait_send()
        for k in range(1, n_req):
            row_copy(lax.rem(mine + k, n_req), mine).wait_send()
    else:
        out_ref[...] = result

    for k in range(n):

        @pl.when((me - k >= 0) & has_right)
        def _():
            gather_copy(me - k, 1).wait_send()

        @pl.when((me + k <= n - 1) & has_left)
        def _():
            gather_copy(me + k, -1).wait_send()

        @pl.when(k > me)
        def _():
            sum_copy(from_left_b, k, 1).wait_send()

        @pl.when(k < me)
        def _():
            sum_copy(from_right_b, k, -1).wait_send()

    @pl.loop(0, pieces)
    def _(index):
        @pl.when(has_right)
        def _():
            line_right(index).wait_send()

        @pl.when(has_left)
        def _():
            line_left(index).wait_send()


def layer_call(n, n_req, x, length, weights, extra):
    rows, width = x.shape
    wq, wo, wu, wd, kc, vc = weights[2], weights[6], weights[10], weights[12], weights[14], weights[15]
    heads = wo.shape[0] // HD
    block = n * rows
    embed = len(extra) > 0
    vmem = pl.BlockSpec(memory_space=pltpu.VMEM)
    hbm = pl.BlockSpec(memory_space=pl.ANY)
    smem = pl.BlockSpec(memory_space=pltpu.SMEM)
    in_hbm = (2, 6, 10, 12, 14, 15)
    specs = [smem, vmem] + [hbm if i in in_hbm else vmem for i in range(len(weights))]
    specs = specs + [vmem] * len(extra)
    full = pltpu.VMEM((block, width), BF16)
    dma = pltpu.SemaphoreType.DMA
    scratch = [pltpu.VMEM(a.shape, BF16) for a in (wq, wo, wu, wd, kc, vc)] + [full] * 12
    scratch = scratch + [
        pltpu.VMEM((block, wq.shape[1]), BF16),
        pltpu.VMEM((block, wo.shape[0]), BF16),
        pltpu.VMEM((block, wu.shape[1]), BF16),
        dma((6,)),
    ]
    scratch = scratch + [dma((n,))] * 3 + [dma((block // 16,))] * 4 + [dma((n,))] * 3
    if embed:
        part = extra[0].shape[1]
        scratch = scratch + [
            pltpu.VMEM(extra[0].shape, BF16),
            pltpu.VMEM((block, part), BF16),
            pltpu.VMEM((n, rows, part), BF16),
            dma((n_req,)),
            dma((n_req,)),
            dma((n,)),
            dma((n,)),
        ]
    return pl.pallas_call(
        functools.partial(layer_kernel, n, n_req, rows, heads, embed),
        out_shape=jax.ShapeDtypeStruct((rows, width), BF16),
        in_specs=specs,
        out_specs=vmem,
        scratch_shapes=scratch,
        compiler_params=pltpu.CompilerParams(
            collective_id=1 if embed else 0,
            has_side_effects=True,
            vmem_limit_bytes=54 * 2**20,
        ),
        cost_estimate=pl.CostEstimate(
            flops=9_000_000_000, bytes_accessed=20_000_000, transcendentals=1_500_000
        ),
        name="first_pass" if embed else "second_pass",
    )(length, x, *weights, *extra)


def shards(
    embeds,
    input_norm_gain,
    input_norm_bias,
    joined_projection_weight,
    joined_projection_bias,
    adapter_down_weight,
    adapter_up_weight,
    attention_out_weight,
    attention_out_bias,
    post_attention_norm_gain,
    post_attention_norm_bias,
    feedforward_up_weight,
    feedforward_up_bias,
    feedforward_down_weight,
    feedforward_down_bias,
    stored_keys,
    stored_values,
    stored_length,
    tenant_first_request,
    accept,
    replacement_token_index,
    word_embedding_table,
):
    n = lax.axis_size("tp")
    req_rank = lax.axis_index("req")
    table_rows = word_embedding_table.shape[0]
    tenant = jnp.sum((req_rank >= tenant_first_request).astype(jnp.int32))
    weights = (
        input_norm_gain[None],
        input_norm_bias[None],
        joined_projection_weight,
        joined_projection_bias[None],
        lax.dynamic_index_in_dim(adapter_down_weight, tenant, 0, keepdims=False),
        lax.dynamic_index_in_dim(adapter_up_weight, tenant, 0, keepdims=False),
        attention_out_weight,
        attention_out_bias[None],
        post_attention_norm_gain[None],
        post_attention_norm_bias[None],
        feedforward_up_weight,
        feedforward_up_bias[None],
        feedforward_down_weight,
        feedforward_down_bias[None],
        stored_keys[0],
        stored_values[0],
    )

    n_req = lax.axis_size("req")
    block = replacement_token_index.shape[0]
    cap = (3 * block // n_req + 15) // 16 * 16
    owner = lax.div(replacement_token_index, jnp.int32(table_rows))
    place = jnp.arange(block)
    earlier = (owner[:, None] == owner[None, :]) & (place[None, :] < place[:, None])
    rank = jnp.sum(earlier.astype(jnp.int32), axis=1)
    pick = (owner * cap + rank)[:, None]

    all_ids = lax.all_gather(replacement_token_index, "req", axis=0)
    local_index = all_ids - req_rank * table_rows
    inside = (local_index >= 0) & (local_index < table_rows)
    before = (place[:, None] < place[None, :]).astype(BF16)
    slot = jnp.dot(inside.astype(BF16), before, preferred_element_type=F32).astype(jnp.int32)
    slot = jnp.where(inside, slot, -1)
    hit = slot[:, None, :] == jnp.arange(cap)[None, :, None]
    wanted = jnp.sum(jnp.where(hit, local_index[:, None, :], 0), axis=2).reshape(-1)
    found = word_embedding_table.at[wanted].get(mode="promise_in_bounds")
    extra = (found, pick, accept[:, None])
    second_in = layer_call(n, n_req, embeds, stored_length, weights, extra)
    return layer_call(n, n_req, second_in, stored_length, weights, ())


def solution(mesh):
    in_specs = (
        P(("req", "tp"), None),
        P(),
        P(),
        P(None, "tp"),
        P("tp"),
        P(),
        P(None, None, "tp"),
        P("tp", None),
        P(),
        P(),
        P(),
        P(None, "tp"),
        P("tp"),
        P("tp", None),
        P(),
        P("req", None, "tp"),
        P("req", None, "tp"),
        P("req"),
        P(),
        P(("req", "tp")),
        P("req"),
        P("req", "tp"),
    )
    out_specs = P(("req", "tp"), None)
    return jax.shard_map(shards, mesh=mesh, in_specs=in_specs, out_specs=out_specs, check_vma=False)
```

```python
import functools

import jax
import jax.numpy as jnp
from jax import lax
from jax.experimental import pallas as pl
from jax.experimental.pallas import tpu as pltpu
from jax.sharding import PartitionSpec as P

H = 16
HD = 128
BLK = 256
EPSILON = 1e-05
F32 = jnp.float32
BF16 = jnp.bfloat16


def norm_rows(values, gain, shift):
    mean = jnp.mean(values, axis=-1, keepdims=True)
    centered = values - mean
    variance = jnp.mean(centered * centered, axis=-1, keepdims=True)
    return (centered * lax.rsqrt(variance + EPSILON) * gain + shift).astype(BF16)


def layer_kernel(n, n_req, rows, heads, embed, *refs):
    refs = iter(refs)
    take = lambda count: [next(refs) for _ in range(count)]
    length_ref, x_ref, in_gain, in_shift, wq_hbm, bq_ref, ad_ref, au_ref = take(8)
    wo_hbm, bo_ref, post_gain, post_shift, wu_hbm, bu_ref, wd_hbm, bd_ref, kc_hbm, vc_hbm = take(10)
    if embed:
        found_ref, pick_ref, accept_ref = take(3)
    (out_ref,) = take(1)
    wq, wo, wu, wd, kc, vc = take(6)
    states, normed, post, attended, part_a, part_b = take(6)
    from_left_a, from_right_a, to_left, to_right, from_left_b, from_right_b = take(6)
    qkv, ctx, hid = take(3)
    load_sem, gat_send_right, gat_send_left, gat_recv = take(4)
    line_send_right, line_send_left, line_recv_left, line_recv_right = take(4)
    sum_send, sum_recv_left, sum_recv_right = take(3)
    if embed:
        landed, picked, replaced, row_send, row_recv, col_send, col_recv = take(7)
    mesh_id = pl.DeviceIdType.MESH
    me = lax.axis_index("tp")
    mine = lax.axis_index("req")
    loads = [
        pltpu.make_async_copy(source, target, load_sem.at[index])
        for index, (source, target) in enumerate(
            ((wq_hbm, wq), (kc_hbm, kc), (vc_hbm, vc), (wo_hbm, wo), (wu_hbm, wu), (wd_hbm, wd))
        )
    ]
    for load in loads:
        load.start()
    has_left = me > 0
    has_right = me < n - 1

    barrier = pltpu.get_barrier_semaphore()
    if embed:
        for k in range(1, n):
            pl.semaphore_signal(
                barrier, inc=1, device_id={"tp": lax.rem(me + k, n)}, device_id_type=mesh_id
            )
        for k in range(1, n_req):
            pl.semaphore_signal(
                barrier, inc=1, device_id={"req": lax.rem(mine + k, n_req)}, device_id_type=mesh_id
            )
    else:

        @pl.when(has_left)
        def _():
            pl.semaphore_signal(barrier, inc=1, device_id={"tp": me - 1}, device_id_type=mesh_id)

        @pl.when(has_right)
        def _():
            pl.semaphore_signal(barrier, inc=1, device_id={"tp": me + 1}, device_id_type=mesh_id)

    def chunk(index):
        return pl.ds(pl.multiple_of(index * rows, rows), rows)

    def zero(buffer):
        buffer[...] = jnp.zeros(buffer.shape, buffer.dtype)

    states[chunk(me), :] = x_ref[...]

    @pl.when(jnp.logical_not(has_left))
    def _():
        zero(from_left_a)

    @pl.when(jnp.logical_not(has_right))
    def _():
        zero(from_right_a)

    if embed:
        pl.semaphore_wait(barrier, n - 1 + n_req - 1)
    else:
        pl.semaphore_wait(barrier, has_left.astype(jnp.int32) + has_right.astype(jnp.int32))

    def gather_copy(index, step):
        sends = gat_send_right if step > 0 else gat_send_left
        return pltpu.make_async_remote_copy(
            src_ref=states.at[chunk(index), :],
            dst_ref=states.at[chunk(index), :],
            send_sem=sends.at[index],
            recv_sem=gat_recv.at[index],
            device_id={"tp": me + step},
            device_id_type=mesh_id,
        )

    def norm_in(index):
        normed[chunk(index), :] = norm_rows(
            states[chunk(index), :].astype(F32), in_gain[...], in_shift[...]
        )

    @pl.when(has_right)
    def _():
        gather_copy(me, 1).start()

    @pl.when(has_left)
    def _():
        gather_copy(me, -1).start()

    if embed:
        cap = found_ref.shape[0] // n_req

        def row_block(index):
            return pl.ds(pl.multiple_of(index * cap, cap), cap)

        def row_copy(peer, source):
            return pltpu.make_async_remote_copy(
                src_ref=found_ref.at[row_block(peer), :],
                dst_ref=landed.at[row_block(source), :],
                send_sem=row_send.at[peer],
                recv_sem=row_recv.at[source],
                device_id={"req": peer},
                device_id_type=mesh_id,
            )

        for k in range(1, n_req):
            row_copy(lax.rem(mine + k, n_req), mine).start()
        landed[row_block(mine), :] = found_ref[row_block(mine), :]

    norm_in(me)
    for k in range(1, n):

        @pl.when(me - k >= 0)
        def _():
            gather_copy(me - k, 1).wait_recv()

            @pl.when(has_right)
            def _():
                gather_copy(me - k, 1).start()

        @pl.when(me + k <= n - 1)
        def _():
            gather_copy(me + k, -1).wait_recv()

            @pl.when(has_left)
            def _():
                gather_copy(me + k, -1).start()

        @pl.when(me - k >= 0)
        def _():
            norm_in(me - k)

        @pl.when(me + k <= n - 1)
        def _():
            norm_in(me + k)

    def columns(index, width):
        return pl.ds(pl.multiple_of(index * width, width), width)

    loads[0].wait()
    low = jnp.dot(normed[...], ad_ref[...], preferred_element_type=F32).astype(BF16)

    @pl.loop(0, wq.shape[1] // 512)
    def _(tile):
        cols = columns(tile, 512)
        joined = jnp.dot(normed[...], wq[:, cols], preferred_element_type=F32)
        joined = joined + jnp.dot(low, au_ref[:, cols], preferred_element_type=F32)
        qkv[:, cols] = (joined + bq_ref[:, cols]).astype(BF16)

    if embed:
        for k in range(1, n_req):
            peer = lax.rem(mine + k, n_req)
            row_copy(peer, peer).wait_recv()
        slots = lax.broadcasted_iota(jnp.int32, (pick_ref.shape[0], landed.shape[0]), 1)
        chosen = jnp.where(slots == pick_ref[...], 1.0, 0.0).astype(BF16)
        picked[...] = jnp.dot(chosen, landed[...], preferred_element_type=F32).astype(BF16)

        def column_copy(peer, source):
            return pltpu.make_async_remote_copy(
                src_ref=picked.at[chunk(peer), :],
                dst_ref=replaced.at[source],
                send_sem=col_send.at[peer],
                recv_sem=col_recv.at[source],
                device_id={"tp": peer},
                device_id_type=mesh_id,
            )

        for k in range(1, n):
            column_copy(lax.rem(me + k, n), me).start()
        replaced[me] = picked[chunk(me), :]

    loads[1].wait()
    loads[2].wait()
    length = length_ref[0]
    cache_rows = kc.shape[0]
    block = qkv.shape[0]
    scale = HD**-0.5

    @pl.loop(0, heads)
    def _(head):
        exponent = jnp.zeros((1, 1), F32) + (me * heads + head + 1).astype(F32) * (-8.0 / H)
        slope = jnp.exp2(exponent)
        query = qkv[:, columns(head * 3, HD)]
        key = qkv[:, columns(head * 3 + 1, HD)]
        value = qkv[:, columns(head * 3 + 2, HD)]
        contract = (((1,), (1,)), ((), ()))
        block_scores = lax.dot_general(query, key, contract, preferred_element_type=F32) * scale
        q_pos = lax.broadcasted_iota(jnp.int32, (block, 1), 0)
        k_pos = lax.broadcasted_iota(jnp.int32, (1, block), 1)
        block_scores = block_scores - slope * jnp.abs(q_pos - k_pos).astype(F32)
        cache_scores = (
            lax.dot_general(query, kc[:, columns(head, HD)], contract, preferred_element_type=F32)
            * scale
        )
        c_pos = lax.broadcasted_iota(jnp.int32, (1, cache_rows), 1)
        cache_scores = cache_scores - slope * (q_pos + length - c_pos).astype(F32)
        cache_scores = jnp.where(c_pos < length, cache_scores, -jnp.inf)
        top = jnp.maximum(
            jnp.max(block_scores, axis=-1, keepdims=True),
            jnp.max(cache_scores, axis=-1, keepdims=True),
        )
        block_weights = jnp.exp(block_scores - top)
        cache_weights = jnp.exp(cache_scores - top)
        total = jnp.sum(block_weights, axis=-1, keepdims=True) + jnp.sum(
            cache_weights, axis=-1, keepdims=True
        )
        mixed = jnp.dot(block_weights.astype(BF16), value, preferred_element_type=F32)
        mixed = mixed + jnp.dot(
            cache_weights.astype(BF16), vc[:, columns(head, HD)], preferred_element_type=F32
        )
        ctx[:, columns(head, HD)] = (mixed / total).astype(BF16)

    loads[3].wait()

    @pl.loop(0, wo.shape[1] // 512)
    def _(tile):
        cols = columns(tile, 512)
        part_a[:, cols] = jnp.dot(ctx[...], wo[:, cols], preferred_element_type=F32).astype(BF16)

    piece_rows = 16
    lag = 5
    pieces = block // piece_rows

    def piece(index):
        return pl.ds(pl.multiple_of(index * piece_rows, piece_rows), piece_rows)

    def line_right(index):
        return pltpu.make_async_remote_copy(
            src_ref=to_right.at[piece(index), :],
            dst_ref=from_left_a.at[piece(index), :],
            send_sem=line_send_right.at[index],
            recv_sem=line_recv_left.at[index],
            device_id={"tp": me + 1},
            device_id_type=mesh_id,
        )

    def line_left(index):
        return pltpu.make_async_remote_copy(
            src_ref=to_left.at[piece(index), :],
            dst_ref=from_right_a.at[piece(index), :],
            send_sem=line_send_left.at[index],
            recv_sem=line_recv_right.at[index],
            device_id={"tp": me - 1},
            device_id_type=mesh_id,
        )

    @pl.loop(0, pieces + lag * (n - 1))
    def _(step):
        right_piece = step - lag * me
        left_piece = step - lag * (n - 1 - me)
        done_piece = step - lag * (n - 1)

        @pl.when((right_piece >= 0) & (right_piece < pieces))
        def _():
            @pl.when(has_left)
            def _():
                line_right(right_piece).wait_recv()

            @pl.when(has_right)
            def _():
                here = piece(right_piece)
                to_right[here, :] = (
                    part_a[here, :].astype(F32) + from_left_a[here, :].astype(F32)
                ).astype(BF16)
                line_right(right_piece).start()

        @pl.when((left_piece >= 0) & (left_piece < pieces))
        def _():
            @pl.when(has_right)
            def _():
                line_left(left_piece).wait_recv()

            @pl.when(has_left)
            def _():
                here = piece(left_piece)
                to_left[here, :] = (
                    part_a[here, :].astype(F32) + from_right_a[here, :].astype(F32)
                ).astype(BF16)
                line_left(left_piece).start()

        @pl.when(done_piece >= 0)
        def _():
            here = piece(done_piece)
            summed = part_a[here, :].astype(F32) + from_left_a[here, :].astype(F32)
            summed = summed + from_right_a[here, :].astype(F32)
            summed = (states[here, :].astype(F32) + summed + bo_ref[...]).astype(BF16)
            attended[here, :] = summed
            post[here, :] = norm_rows(summed.astype(F32), post_gain[...], post_shift[...])

    loads[4].wait()

    @pl.loop(0, wu.shape[1] // 512)
    def _(tile):
        cols = columns(tile, 512)
        inner = jnp.dot(post[...], wu[:, cols], preferred_element_type=F32) + bu_ref[:, cols]
        hid[:, cols] = jax.nn.gelu(inner, approximate=True).astype(BF16)

    loads[5].wait()

    @pl.loop(0, wd.shape[1] // 512)
    def _(tile):
        cols = columns(tile, 512)
        part_b[:, cols] = jnp.dot(hid[...], wd[:, cols], preferred_element_type=F32).astype(BF16)

    def sum_copy(landing, index, step):
        recvs = sum_recv_left if step > 0 else sum_recv_right
        return pltpu.make_async_remote_copy(
            src_ref=part_b.at[chunk(index), :],
            dst_ref=landing.at[chunk(index), :],
            send_sem=sum_send.at[index],
            recv_sem=recvs.at[index],
            device_id={"tp": me + step},
            device_id_type=mesh_id,
        )

    def add_in(landing, index):
        part_b[chunk(index), :] = (
            part_b[chunk(index), :].astype(F32) + landing[chunk(index), :].astype(F32)
        ).astype(BF16)

    for k in range(n - 1):
        right_index = n - 1 - k
        left_index = k

        @pl.when(right_index > me)
        def _():
            @pl.when(has_left)
            def _():
                sum_copy(from_left_b, right_index, 1).wait_recv()
                add_in(from_left_b, right_index)

            sum_copy(from_left_b, right_index, 1).start()

        @pl.when(left_index < me)
        def _():
            @pl.when(has_right)
            def _():
                sum_copy(from_right_b, left_index, -1).wait_recv()
                add_in(from_right_b, left_index)

            sum_copy(from_right_b, left_index, -1).start()

    @pl.when(has_left)
    def _():
        sum_copy(from_left_b, me, 1).wait_recv()
        add_in(from_left_b, me)

    @pl.when(has_right)
    def _():
        sum_copy(from_right_b, me, -1).wait_recv()
        add_in(from_right_b, me)

    result = (
        attended[chunk(me), :].astype(F32) + part_b[chunk(me), :].astype(F32) + bd_ref[...]
    ).astype(BF16)
    if embed:
        width = replaced.shape[2]
        for k in range(1, n):
            peer = lax.rem(me + k, n)
            column_copy(peer, peer).wait_recv()
        for k in range(n):
            cols = slice(k * width, (k + 1) * width)
            out_ref[:, cols] = jnp.where(accept_ref[...] == 1, replaced[k], result[:, cols])
        for k in range(1, n):
            column_copy(lax.rem(me + k, n), me).wait_send()
        for k in range(1, n_req):
            row_copy(lax.rem(mine + k, n_req), mine).wait_send()
    else:
        out_ref[...] = result

    for k in range(n):

        @pl.when((me - k >= 0) & has_right)
        def _():
            gather_copy(me - k, 1).wait_send()

        @pl.when((me + k <= n - 1) & has_left)
        def _():
            gather_copy(me + k, -1).wait_send()

        @pl.when(k > me)
        def _():
            sum_copy(from_left_b, k, 1).wait_send()

        @pl.when(k < me)
        def _():
            sum_copy(from_right_b, k, -1).wait_send()

    @pl.loop(0, pieces)
    def _(index):
        @pl.when(has_right)
        def _():
            line_right(index).wait_send()

        @pl.when(has_left)
        def _():
            line_left(index).wait_send()


def layer_call(n, n_req, x, length, weights, extra):
    rows, width = x.shape
    wq, wo, wu, wd, kc, vc = weights[2], weights[6], weights[10], weights[12], weights[14], weights[15]
    heads = wo.shape[0] // HD
    block = n * rows
    embed = len(extra) > 0
    vmem = pl.BlockSpec(memory_space=pltpu.VMEM)
    hbm = pl.BlockSpec(memory_space=pl.ANY)
    smem = pl.BlockSpec(memory_space=pltpu.SMEM)
    in_hbm = (2, 6, 10, 12, 14, 15)
    specs = [smem, vmem] + [hbm if i in in_hbm else vmem for i in range(len(weights))]
    specs = specs + [vmem] * len(extra)
    full = pltpu.VMEM((block, width), BF16)
    dma = pltpu.SemaphoreType.DMA
    scratch = [pltpu.VMEM(a.shape, BF16) for a in (wq, wo, wu, wd, kc, vc)] + [full] * 12
    scratch = scratch + [
        pltpu.VMEM((block, wq.shape[1]), BF16),
        pltpu.VMEM((block, wo.shape[0]), BF16),
        pltpu.VMEM((block, wu.shape[1]), BF16),
        dma((6,)),
    ]
    scratch = scratch + [dma((n,))] * 3 + [dma((block // 16,))] * 4 + [dma((n,))] * 3
    if embed:
        part = extra[0].shape[1]
        scratch = scratch + [
            pltpu.VMEM(extra[0].shape, BF16),
            pltpu.VMEM((block, part), BF16),
            pltpu.VMEM((n, rows, part), BF16),
            dma((n_req,)),
            dma((n_req,)),
            dma((n,)),
            dma((n,)),
        ]
    return pl.pallas_call(
        functools.partial(layer_kernel, n, n_req, rows, heads, embed),
        out_shape=jax.ShapeDtypeStruct((rows, width), BF16),
        in_specs=specs,
        out_specs=vmem,
        scratch_shapes=scratch,
        compiler_params=pltpu.CompilerParams(
            collective_id=1 if embed else 0,
            has_side_effects=True,
            vmem_limit_bytes=54 * 2**20,
        ),
        cost_estimate=pl.CostEstimate(
            flops=9_000_000_000, bytes_accessed=20_000_000, transcendentals=1_500_000
        ),
        name="first_pass" if embed else "second_pass",
    )(length, x, *weights, *extra)


def shards(
    embeds,
    input_norm_gain,
    input_norm_bias,
    joined_projection_weight,
    joined_projection_bias,
    adapter_down_weight,
    adapter_up_weight,
    attention_out_weight,
    attention_out_bias,
    post_attention_norm_gain,
    post_attention_norm_bias,
    feedforward_up_weight,
    feedforward_up_bias,
    feedforward_down_weight,
    feedforward_down_bias,
    stored_keys,
    stored_values,
    stored_length,
    tenant_first_request,
    accept,
    replacement_token_index,
    word_embedding_table,
):
    n = lax.axis_size("tp")
    req_rank = lax.axis_index("req")
    table_rows = word_embedding_table.shape[0]
    tenant = jnp.sum((req_rank >= tenant_first_request).astype(jnp.int32))
    weights = (
        input_norm_gain[None],
        input_norm_bias[None],
        joined_projection_weight,
        joined_projection_bias[None],
        lax.dynamic_index_in_dim(adapter_down_weight, tenant, 0, keepdims=False),
        lax.dynamic_index_in_dim(adapter_up_weight, tenant, 0, keepdims=False),
        attention_out_weight,
        attention_out_bias[None],
        post_attention_norm_gain[None],
        post_attention_norm_bias[None],
        feedforward_up_weight,
        feedforward_up_bias[None],
        feedforward_down_weight,
        feedforward_down_bias[None],
        stored_keys[0],
        stored_values[0],
    )

    n_req = lax.axis_size("req")
    block = replacement_token_index.shape[0]
    cap = (3 * block // n_req + 15) // 16 * 16
    owner = lax.div(replacement_token_index, jnp.int32(table_rows))
    place = jnp.arange(block)
    earlier = (owner[:, None] == owner[None, :]) & (place[None, :] < place[:, None])
    rank = jnp.sum(earlier.astype(jnp.int32), axis=1)
    pick = (owner * cap + rank)[:, None]

    all_ids = lax.all_gather(replacement_token_index, "req", axis=0)
    local_index = all_ids - req_rank * table_rows
    inside = (local_index >= 0) & (local_index < table_rows)
    before = (place[:, None] < place[None, :]).astype(BF16)
    slot = jnp.dot(inside.astype(BF16), before, preferred_element_type=F32).astype(jnp.int32)
    slot = jnp.where(inside, slot, -1)
    hit = slot[:, None, :] == jnp.arange(cap)[None, :, None]
    wanted = jnp.sum(jnp.where(hit, local_index[:, None, :], 0), axis=2).reshape(-1)
    found = word_embedding_table.at[wanted].get(mode="promise_in_bounds")
    extra = (found, pick, accept[:, None])
    second_in = layer_call(n, n_req, embeds, stored_length, weights, extra)
    return layer_call(n, n_req, second_in, stored_length, weights, ())


def solution(mesh):
    in_specs = (
        P(("req", "tp"), None),
        P(),
        P(),
        P(None, "tp"),
        P("tp"),
        P(),
        P(None, None, "tp"),
        P("tp", None),
        P(),
        P(),
        P(),
        P(None, "tp"),
        P("tp"),
        P("tp", None),
        P(),
        P("req", None, "tp"),
        P("req", None, "tp"),
        P("req"),
        P(),
        P(("req", "tp")),
        P("req"),
        P("req", "tp"),
    )
    out_specs = P(("req", "tp"), None)
    return jax.shard_map(shards, mesh=mesh, in_specs=in_specs, out_specs=out_specs, check_vma=False)
```
